32 devices in a mesh: row: 4 (over y, x), col: 8 (over z, core).
Axes of the slice: x: 2, y: 2, z: 4, core: 2. Of those that a mesh axis runs over, the one named last changes fastest.
Arguments:
- sigma_anc: bfloat16 [8, 640, 5120], P(None, 'col', 'row'), may hold values from -6 to 6
- owner: int32 [8], replicated, may hold values from 0 to 7, as said below
- structure: int32 [8, 4], replicated, may hold values from 0 to 7, as said below
- factor: bfloat16 [8, 2560, 640], P('col', 'row'), may hold values from -0.125 to 0.125
- diag_inv: float32 [8, 640, 640], P('col', None, 'row'), may hold values from -6 to 6
Outputs:
- offdiag: bfloat16 [8, 2560, 640], P('col', 'row')
- diagblock: float32 [8, 640, 640], P('col', None, 'row')
The draws below stay inside these ranges and needn't reach their ends.
Inputs may be any that keep to these rules, and one draw needn't show every extreme that they name: owner maps each group of 2 ancestors, j // 2 equal, one to one onto the stored columns of the same group. `structure`: entry a of every supernode's list lies between a * 2 and (a + 1) * 2 - 1.
All inputs are finite; a program needn't handle non-finite values.
Results may differ from the reference program's by a relative error of at most 0.014.
Values may be sent and summed in bfloat16 or wider, within the bound.
A program may use at most 64 MiB of HBM per device.

```python
import jax
import jax.numpy as jnp
from jax import lax

B = 640
NA = 8
GROUP = 2
S = 4
NS = 8


def draw_owner(key, part):
    group_keys = jax.random.split(jax.random.fold_in(key, 11), NA // GROUP)
    shuffled = jax.vmap(lambda single: jax.random.permutation(single, GROUP))(group_keys)
    starts = lax.broadcasted_iota(jnp.int32, (NA // GROUP, GROUP), 0) * GROUP
    return (shuffled.astype(jnp.int32) + starts).reshape(NA).astype(jnp.int32)


def draw_structure(key, part):
    key_one, key_two = jax.random.split(jax.random.fold_in(key, 7))
    first_pick = jax.random.randint(key_one, (NS, S), 0, GROUP)
    second_pick = jax.random.randint(key_two, (NS, S), 0, GROUP)
    offset = jnp.minimum(first_pick, second_pick)
    row_ids = lax.broadcasted_iota(jnp.int32, (NS, S), 0)
    slot_ids = lax.broadcasted_iota(jnp.int32, (NS, S), 1)
    offset = jnp.where((row_ids == NS - 1) & (slot_ids == S - 1), GROUP - 1, offset)
    offset = jnp.where((row_ids == 0) & (slot_ids == 0), 0, offset)
    return (slot_ids * GROUP + offset).astype(jnp.int32)


def level_of(rng, dims, pieces, low, high):
    gain, own = 1.0, jax.random.fold_in(rng, 6)
    for position, parts in pieces:
        draws = jnp.exp(jax.random.uniform(jax.random.fold_in(own, position), (parts,), jnp.float32, low / len(pieces), high / len(pieces)))
        gain = gain * jnp.repeat(draws, dims[position] // parts).reshape([-1 if axis == position else 1 for axis in range(len(dims))])
    return gain


def gaussian(key, shape, scale, reach, pieces=(), held_as=jnp.bfloat16):
    result = scale * jax.random.normal(key, shape, jnp.float32)
    if pieces:
        result = result * level_of(key, shape, pieces, -0.22, 0.18)
    return jnp.clip(result, -reach, reach).astype(held_as)


def setup_inputs(seed: int = 0) -> dict:
    splits = jax.random.split(jax.random.key(seed), 6)
    return {
        "sigma_anc": gaussian(splits[0], (NA, B, NA * B), 1.0, 6.0, ((1, 8), (2, 4))),
        "owner": draw_owner(jax.random.fold_in(splits[5], 71), 0),
        "structure": draw_structure(jax.random.fold_in(splits[5], 71), 0),
        "factor": gaussian(splits[3], (NS, S * B, B), (S * B) ** -0.5, 0.125, ((0, 8), (1, 4))),
        "diag_inv": gaussian(splits[4], (NS, B, B), 1.0, 6.0, ((0, 8), (2, 4)), jnp.float32),
    }


def reference(sigma_anc, owner, structure, factor, diag_inv):
    blocks = sigma_anc.reshape(NA, B, NA, B)

    def per_supernode(inputs):
        listed, factor_panel, inverse_diag = inputs
        stored = jnp.take(owner, listed)
        picked = jnp.take(blocks, stored, axis=2)
        picked = jnp.take(picked, listed, axis=0)
        panel_blocks = factor_panel.reshape(S, B, B).astype(jnp.float32)
        slot_terms = jnp.einsum('aibj,bjk->baik', picked.astype(jnp.float32), panel_blocks)
        slot_terms = lax.optimization_barrier(slot_terms.astype(jnp.bfloat16)).astype(jnp.float32)
        offdiag = (-jnp.sum(slot_terms, axis=0)).reshape(S * B, B).astype(jnp.bfloat16)
        products = lax.dot_general(factor_panel, offdiag, (((0,), (0,)), ((), ())), preferred_element_type=jnp.float32)
        return offdiag, inverse_diag - products

    offdiag, diagblock = lax.map(per_supernode, (structure, factor, diag_inv))
    return offdiag, diagblock
```

```python
import functools

import jax
import jax.numpy as jnp
from jax import lax
from jax.experimental import pallas as pl
from jax.experimental.pallas import tpu as pltpu
from jax.sharding import PartitionSpec as P

MESH = pl.DeviceIdType.MESH


def gather_kernel(owner_ref, struct_ref, sig_ref, out_ref):
    r = lax.axis_index("row")
    rows = sig_ref.shape[1]
    width = out_ref.shape[2]
    groups = sig_ref.shape[2] // width

    @pl.loop(0, struct_ref.shape[0])
    def _(k):
        column = owner_ref[struct_ref[k, r]] - r * groups
        lanes = pl.ds(pl.multiple_of(column * width, 128), width)
        for a in range(struct_ref.shape[1]):
            out_ref[k, a * rows : (a + 1) * rows, :] = sig_ref[struct_ref[k, a], :, lanes]


def kernel(
    nr, nc, outgoing, full_ref, fac_ref, diag_ref, off_ref, out_ref,
    recv, terms, rs_recv, total, pieces, p_recv,
    a_send, a_recv, b_send, b_recv, d_send, d_recv,
):
    r = lax.axis_index("row")
    c = lax.axis_index("col")
    rows = fac_ref.shape[1]
    width = full_ref.shape[1]
    strip = width // nr

    def flipped(s):
        result = 0
        bit = 1
        while bit < nc:
            mine = (c // bit) % 2
            other = (s // bit) % 2
            result = result + bit * (mine + other - 2 * mine * other)
            bit *= 2
        return result

    barrier = pltpu.get_barrier_semaphore()
    for d in range(1, nc):
        pl.semaphore_signal(barrier, inc=1, device_id=(r, lax.rem(c + d, nc)), device_id_type=MESH)
    for d in range(1, nr):
        pl.semaphore_signal(barrier, inc=1, device_id=(lax.rem(r + d, nr), c), device_id_type=MESH)

    def sigma_copy(s):
        k = flipped(s)
        return pltpu.make_async_remote_copy(
            src_ref=outgoing.at[k], dst_ref=recv.at[c], send_sem=a_send.at[k], recv_sem=a_recv.at[c],
            device_id=(r, k), device_id_type=MESH,
        )

    def sigma_wait(k):
        pltpu.make_async_remote_copy(
            src_ref=outgoing.at[k], dst_ref=recv.at[k], send_sem=a_send.at[k], recv_sem=a_recv.at[k],
            device_id=(r, k), device_id_type=MESH,
        ).wait_recv()

    def term_copy(i, d):
        to = lax.rem(r + d, nr)
        return pltpu.make_async_remote_copy(
            src_ref=terms.at[i, pl.ds(to * rows, rows)], dst_ref=rs_recv.at[d - 1, i],
            send_sem=b_send.at[d - 1, i], recv_sem=b_recv.at[d - 1, i],
            device_id=(to, c), device_id_type=MESH,
        )

    def piece_copy(d):
        to = lax.rem(r + d, nr)
        return pltpu.make_async_remote_copy(
            src_ref=pieces.at[d - 1], dst_ref=p_recv.at[d - 1],
            send_sem=d_send.at[d - 1], recv_sem=d_recv.at[d - 1],
            device_id=(to, c), device_id_type=MESH,
        )

    pl.semaphore_wait(barrier, nc - 1 + nr - 1)

    @pl.loop(0, nc - 1)
    def _(t):
        sigma_copy(nc - 1 - t).start()

    total[...] = jnp.zeros_like(total)

    def finish(s):
        i = flipped(s)
        for d in range(1, nr):
            term_copy(i, d).wait_recv()
        acc = terms[i, pl.ds(r * rows, rows)].astype(jnp.float32)
        for d in range(1, nr):
            acc = acc + rs_recv[d - 1, i].astype(jnp.float32)
        block = (-acc).astype(jnp.bfloat16)
        off_ref[i] = block
        total[...] += lax.dot_general(
            block, fac_ref[i], (((0,), (0,)), ((), ())), preferred_element_type=jnp.float32
        )

    @pl.loop(0, nc)
    def _(s):
        i = flipped(s)

        @pl.when(s > 0)
        def _():
            sigma_wait(i)

        def multiply(block):
            product = jnp.dot(block, full_ref[...], preferred_element_type=jnp.float32)
            terms[i] = product.astype(jnp.bfloat16)

        @pl.when(s == 0)
        def _():
            multiply(outgoing[c])

        @pl.when(s > 0)
        def _():
            multiply(recv[i])

        for d in range(1, nr):
            term_copy(i, d).start()

        @pl.when(s > 0)
        def _():
            finish(s - 1)

    finish(nc - 1)
    for d in range(1, nr):
        to = lax.rem(r + d, nr)
        pieces[d - 1] = total[pl.ds(pl.multiple_of(to * strip, 8), strip), :].astype(jnp.bfloat16)
        piece_copy(d).start()
    acc = total[pl.ds(pl.multiple_of(r * strip, 8), strip), :]
    for d in range(1, nr):
        piece_copy(d).wait_recv()
        acc = acc + p_recv[d - 1].astype(jnp.float32)
    out_ref[...] = diag_ref[...] - acc

    @pl.loop(1, nc)
    def _(s):
        sigma_copy(s).wait_send()

    @pl.loop(0, nc)
    def _(i):
        for d in range(1, nr):
            term_copy(i, d).wait_send()

    for d in range(1, nr):
        piece_copy(d).wait_send()


def body(nr, nc, sigma_anc, owner, structure, factor, diag_inv):
    rows = sigma_anc.shape[1]
    width = factor.shape[2]
    strip = width // nr
    full = factor[0]
    cut = full.reshape(nc, rows, width)
    padded = -(-rows // 16) * 16
    if padded != rows:
        extra = (0, 0), (0, padded - rows), (0, 0)
        sigma_anc, cut = jnp.pad(sigma_anc, extra), jnp.pad(cut, extra)
    vmem = pl.BlockSpec(memory_space=pltpu.VMEM)
    smem = pl.BlockSpec(memory_space=pltpu.SMEM)
    dma = pltpu.SemaphoreType.DMA
    outgoing = pl.pallas_call(
        gather_kernel,
        out_shape=jax.ShapeDtypeStruct((nc, nr * padded, width), jnp.bfloat16),
        in_specs=[smem, smem, vmem],
        out_specs=vmem,
        compiler_params=pltpu.CompilerParams(vmem_limit_bytes=32 * 1024 * 1024),
    )(owner, structure, sigma_anc)
    off, diag = pl.pallas_call(
        functools.partial(kernel, nr, nc),
        out_shape=(
            jax.ShapeDtypeStruct((nc, padded, width), jnp.bfloat16),
            jax.ShapeDtypeStruct((strip, width), jnp.float32),
        ),
        in_specs=[vmem, vmem, vmem, vmem],
        out_specs=(vmem, vmem),
        scratch_shapes=[
            pltpu.VMEM((nc, nr * padded, width), jnp.bfloat16),
            pltpu.VMEM((nc, nr * padded, width), jnp.bfloat16),
            pltpu.VMEM((nr - 1, nc, padded, width), jnp.bfloat16),
            pltpu.VMEM((width, width), jnp.float32),
            pltpu.VMEM((nr - 1, strip, width), jnp.bfloat16),
            pltpu.VMEM((nr - 1, strip, width), jnp.bfloat16),
            dma((nc,)), dma((nc,)), dma((nr - 1, nc)), dma((nr - 1, nc)), dma((nr - 1,)), dma((nr - 1,)),
        ],
        compiler_params=pltpu.CompilerParams(
            collective_id=0, has_side_effects=True, vmem_limit_bytes=60 * 1024 * 1024
        ),
    )(outgoing, full, cut, diag_inv[0].T)
    return off[:, :rows].reshape(1, width, width), diag.T[None]


def solution(mesh):
    return jax.shard_map(
        functools.partial(body, mesh.shape["row"], mesh.shape["col"]),
        mesh=mesh,
        in_specs=(P(None, "col", "row"), P(), P(), P("col", "row", None), P("col", None, "row")),
        out_specs=(P("col", "row", None), P("col", None, "row")),
        check_vma=False,
    )
```

```python
import functools

import jax
import jax.numpy as jnp
from jax import lax
from jax.experimental import pallas as pl
from jax.experimental.pallas import tpu as pltpu
from jax.sharding import PartitionSpec as P

MESH = pl.DeviceIdType.MESH


def gather_kernel(owner_ref, struct_ref, sig_ref, out_ref):
    r = lax.axis_index("row")
    rows = sig_ref.shape[1]
    width = out_ref.shape[2]
    groups = sig_ref.shape[2] // width

    @pl.loop(0, struct_ref.shape[1])
    def _(k):
        column = owner_ref[struct_ref[r, k]] - r * groups
        lanes = pl.ds(pl.multiple_of(column * width, 128), width)
        for a in range(struct_ref.shape[0]):
            out_ref[k, a * rows : (a + 1) * rows, :] = sig_ref[struct_ref[a, k], :, lanes]


def direct_kernel(
    nr, nc, outgoing, full_ref, fac_ref, diag_ref, off_ref, out_ref,
    recv, terms, rs_recv, total, pieces, p_recv,
    a_send, a_recv, b_send, b_recv, d_send, d_recv,
):
    r = lax.axis_index("row")
    c = lax.axis_index("col")
    rows = fac_ref.shape[1]
    width = full_ref.shape[1]
    strip = width // nr

    def flipped(s):
        result = 0
        bit = 1
        while bit < nc:
            mine = (c // bit) % 2
            other = (s // bit) % 2
            result = result + bit * (mine + other - 2 * mine * other)
            bit *= 2
        return result

    barrier = pltpu.get_barrier_semaphore()
    for d in range(1, nc):
        pl.semaphore_signal(barrier, inc=1, device_id=(r, lax.rem(c + d, nc)), device_id_type=MESH)
    for d in range(1, nr):
        pl.semaphore_signal(barrier, inc=1, device_id=(lax.rem(r + d, nr), c), device_id_type=MESH)

    def sigma_copy(s):
        k = flipped(s)
        return pltpu.make_async_remote_copy(
            src_ref=outgoing.at[k], dst_ref=recv.at[c], send_sem=a_send.at[k], recv_sem=a_recv.at[c],
            device_id=(r, k), device_id_type=MESH,
        )

    def sigma_wait(k):
        pltpu.make_async_remote_copy(
            src_ref=outgoing.at[k], dst_ref=recv.at[k], send_sem=a_send.at[k], recv_sem=a_recv.at[k],
            device_id=(r, k), device_id_type=MESH,
        ).wait_recv()

    def term_copy(i, d):
        to = lax.rem(r + d, nr)
        return pltpu.make_async_remote_copy(
            src_ref=terms.at[i, pl.ds(to * rows, rows)], dst_ref=rs_recv.at[d - 1, i],
            send_sem=b_send.at[d - 1, i], recv_sem=b_recv.at[d - 1, i],
            device_id=(to, c), device_id_type=MESH,
        )

    def piece_copy(d):
        to = lax.rem(r + d, nr)
        return pltpu.make_async_remote_copy(
            src_ref=pieces.at[d - 1], dst_ref=p_recv.at[d - 1],
            send_sem=d_send.at[d - 1], recv_sem=d_recv.at[d - 1],
            device_id=(to, c), device_id_type=MESH,
        )

    pl.semaphore_wait(barrier, nc - 1 + nr - 1)

    @pl.loop(0, nc - 1)
    def _(t):
        sigma_copy(nc - 1 - t).start()

    total[...] = jnp.zeros_like(total)

    def finish(s):
        i = flipped(s)
        for d in range(1, nr):
            term_copy(i, d).wait_recv()
        acc = terms[i, pl.ds(r * rows, rows)].astype(jnp.float32)
        for d in range(1, nr):
            acc = acc + rs_recv[d - 1, i].astype(jnp.float32)
        block = (-acc).astype(jnp.bfloat16)
        off_ref[i] = block
        total[...] += lax.dot_general(
            block, fac_ref[i], (((0,), (0,)), ((), ())), preferred_element_type=jnp.float32
        )

    @pl.loop(0, nc)
    def _(s):
        i = flipped(s)

        @pl.when(s > 0)
        def _():
            sigma_wait(i)

        def multiply(block):
            product = jnp.dot(block, full_ref[...], preferred_element_type=jnp.float32)
            terms[i] = product.astype(jnp.bfloat16)

        @pl.when(s == 0)
        def _():
            multiply(outgoing[c])

        @pl.when(s > 0)
        def _():
            multiply(recv[i])

        for d in range(1, nr):
            term_copy(i, d).start()

        @pl.when(s > 0)
        def _():
            finish(s - 1)

    finish(nc - 1)
    for d in range(1, nr):
        to = lax.rem(r + d, nr)
        pieces[d - 1] = total[pl.ds(pl.multiple_of(to * strip, 8), strip), :].astype(jnp.bfloat16)
        piece_copy(d).start()
    acc = total[pl.ds(pl.multiple_of(r * strip, 8), strip), :]
    for d in range(1, nr):
        piece_copy(d).wait_recv()
        acc = acc + p_recv[d - 1].astype(jnp.float32)
    out_ref[...] = diag_ref[...] - acc

    @pl.loop(1, nc)
    def _(s):
        sigma_copy(s).wait_send()

    @pl.loop(0, nc)
    def _(i):
        for d in range(1, nr):
            term_copy(i, d).wait_send()

    for d in range(1, nr):
        piece_copy(d).wait_send()


CHUNKS = 4


def line_kernel(
    nr, nc, outgoing, full_ref, fac_ref, diag_ref, off_ref, out_ref,
    panels, sent_rows, terms, rs_recv, stage, total, pieces, p_recv,
    z_send, s_send, g_recv, a_send, a_recv, b_send, b_recv, o_send, o_recv, d_send, d_recv,
):
    r = lax.axis_index("row")
    c = lax.axis_index("col")
    rows = fac_ref.shape[1]
    width = full_ref.shape[1]
    strip = width // nr
    depth = width // CHUNKS
    z, q = c // 2, c % 2
    half = z // 2
    mid, end = 2 * (1 + half), 6 * half
    mid_far, end_far = 2 * (2 - half), 6 * (1 - half)
    here = 2 * z
    sibling = here + 1 - q
    is_end = 1 - (z + 1) // 2 % 2

    barrier = pltpu.get_barrier_semaphore()
    for d in range(1, nc):
        pl.semaphore_signal(barrier, inc=1, device_id=(r, lax.rem(c + d, nc)), device_id_type=MESH)
    for d in range(1, nr):
        pl.semaphore_signal(barrier, inc=1, device_id=(lax.rem(r + d, nr), c), device_id_type=MESH)

    def panel_copy(k, ch, to, sem):
        part = panels.at[k, pl.ds(ch * depth, depth)]
        return pltpu.make_async_remote_copy(
            src_ref=part, dst_ref=part, send_sem=sem.at[k, ch], recv_sem=g_recv.at[k, ch],
            device_id=(r, to), device_id_type=MESH,
        )

    def to_sibling(k, ch):
        return panel_copy(k, ch, sibling, s_send)

    def take(k, ch, onward=None):
        panel_copy(k, ch, sibling, s_send).wait_recv()
        if onward is not None:
            panel_copy(k, ch, onward, z_send).start()
        to_sibling(k, ch).start()

    def from_sibling(k):
        @pl.loop(0, CHUNKS)
        def _(ch):
            to_sibling(k, ch).wait_recv()

    def rows_copy(t):
        return pltpu.make_async_remote_copy(
            src_ref=outgoing.at[mid + t], dst_ref=sent_rows.at[q], send_sem=a_send.at[t], recv_sem=a_recv.at[q],
            device_id=(r, mid + t), device_id_type=MESH,
        )

    def rows_wait(t):
        pltpu.make_async_remote_copy(
            src_ref=outgoing.at[mid + t], dst_ref=sent_rows.at[t], send_sem=a_send.at[t], recv_sem=a_recv.at[t],
            device_id=(r, end + t), device_id_type=MESH,
        ).wait_recv()

    def term_copy(job, d):
        to = lax.rem(r + d, nr)
        return pltpu.make_async_remote_copy(
            src_ref=terms.at[job, pl.ds(to * rows, rows)], dst_ref=rs_recv.at[d - 1, job],
            send_sem=b_send.at[d - 1, job], recv_sem=b_recv.at[d - 1, job],
            device_id=(to, c), device_id_type=MESH,
        )

    def tile_copy(job, k):
        return pltpu.make_async_remote_copy(
            src_ref=stage.at[job], dst_ref=off_ref.at[c], send_sem=o_send.at[job], recv_sem=o_recv.at[c],
            device_id=(r, k), device_id_type=MESH,
        )

    def tile_wait(i):
        pltpu.make_async_remote_copy(
            src_ref=stage.at[0], dst_ref=off_ref.at[i], send_sem=o_send.at[0], recv_sem=o_recv.at[i],
            device_id=(r, i), device_id_type=MESH,
        ).wait_recv()

    def piece_copy(d):
        to = lax.rem(r + d, nr)
        return pltpu.make_async_remote_copy(
            src_ref=pieces.at[d - 1], dst_ref=p_recv.at[d - 1],
            send_sem=d_send.at[d - 1], recv_sem=d_recv.at[d - 1],
            device_id=(to, c), device_id_type=MESH,
        )

    def multiply(job, left, right):
        product = jnp.dot(left[...], right[...], preferred_element_type=jnp.float32)
        terms[job] = product.astype(jnp.bfloat16)
        for d in range(1, nr):
            term_copy(job, d).start()

    def issue(group, base):
        @pl.loop(0, 2)
        def _(t):
            k = base + (q + t) % 2

            @pl.when(t == 1)
            def _():
                from_sibling(k)

            multiply(2 * group + t, outgoing.at[k], panels.at[k])

    def summed(job):
        for d in range(1, nr):
            term_copy(job, d).wait_recv()
        acc = terms[job, pl.ds(pl.multiple_of(r * rows, 16), rows)].astype(jnp.float32)
        for d in range(1, nr):
            acc = acc + rs_recv[d - 1, job].astype(jnp.float32)
        return (-acc).astype(jnp.bfloat16)

    def deliver(group, base):
        @pl.loop(0, 2)
        def _(t):
            job = 2 * group + t
            stage[job] = summed(job)
            tile_copy(job, base + (q + t) % 2).start()

    def deliver_own():
        off_ref[c] = summed(0)
        stage[1] = summed(1)
        tile_copy(1, sibling).start()

    panels[c] = full_ref[...]
    pl.semaphore_wait(barrier, nc - 1 + nr - 1)

    @pl.loop(0, CHUNKS)
    def _(ch):
        panel_copy(c, ch, (1 - is_end) * mid_far + is_end * mid + q, z_send).start()
        to_sibling(c, ch).start()

    issue(0, here)

    @pl.when(is_end == 1)
    def _():
        @pl.loop(0, CHUNKS)
        def _(ch):
            panel_copy(c, ch, mid + q, z_send).wait_send()

        @pl.loop(0, 2)
        def _(t):
            rows_copy(t).start()

        @pl.loop(0, CHUNKS)
        def _(ch):
            take(mid_far + q, ch)

    @pl.when(is_end == 0)
    def _():
        @pl.loop(0, CHUNKS)
        def _(ch):
            take(end + q, ch, mid_far + q)
            take(mid_far + q, ch, end + q)

        issue(1, end)

    issue(2, mid_far)
    deliver_own()

    @pl.when(is_end == 1)
    def _():
        deliver(2, mid_far)

        @pl.loop(0, CHUNKS)
        def _(ch):
            take(end_far + q, ch)

    @pl.when(is_end == 0)
    def _():
        take(end_far + q, 0, end + q)
        take(end_far + q, 1, end + q)
        deliver(1, end)
        take(end_far + q, 2, end + q)
        deliver(2, mid_far)
        take(end_far + q, 3, end + q)

    issue(4, end_far)

    @pl.when(is_end == 0)
    def _():
        @pl.loop(0, 2)
        def _(t):
            rows_wait(t)
            multiply(6 + t, sent_rows.at[t], panels.at[c])

    deliver(4, end_far)

    @pl.when(is_end == 0)
    def _():
        @pl.loop(0, 2)
        def _(t):
            off_ref[end + t] = summed(6 + t)

    def partial(start):
        part = pl.ds(start, nc // 2)
        return lax.dot_general(
            off_ref[part].reshape(width // 2, width), fac_ref[part].reshape(width // 2, width),
            (((0,), (0,)), ((), ())), preferred_element_type=jnp.float32,
        )

    tile_wait(sibling)

    @pl.when(is_end == 1)
    def _():
        tile_wait(mid)
        tile_wait(mid + 1)

    total[...] = partial(half * (nc // 2))
    for i in (mid_far, mid_far + 1, end_far, end_far + 1):
        tile_wait(i)
    total[...] += partial((1 - half) * (nc // 2))

    for d in range(1, nr):
        to = lax.rem(r + d, nr)
        pieces[d - 1] = total[pl.ds(pl.multiple_of(to * strip, 8), strip), :].astype(jnp.bfloat16)
        piece_copy(d).start()
    acc = total[pl.ds(pl.multiple_of(r * strip, 8), strip), :]
    for d in range(1, nr):
        piece_copy(d).wait_recv()
        acc = acc + p_recv[d - 1].astype(jnp.float32)
    out_ref[...] = diag_ref[...] - acc

    def sent(base):
        @pl.loop(0, CHUNKS)
        def _(ch):
            panel_copy(base, ch, sibling, z_send).wait_send()

    def shared(base):
        @pl.loop(0, CHUNKS)
        def _(ch):
            to_sibling(base, ch).wait_send()

    def done(job):
        for d in range(1, nr):
            term_copy(job, d).wait_send()

    for k in (c, mid_far + q, end_far + q):
        shared(k)
    tile_copy(1, sibling).wait_send()
    for group in (2, 4):
        for t in range(2):
            tile_copy(2 * group + t, sibling).wait_send()
    for job in (0, 1, 4, 5, 8, 9):
        done(job)

    @pl.when(is_end == 1)
    def _():
        for t in range(2):
            rows_copy(t).wait_send()

    @pl.when(is_end == 0)
    def _():
        for k in (c, end + q, mid_far + q, end_far + q):
            sent(k)
        shared(end + q)
        for t in range(2):
            tile_copy(2 + t, sibling).wait_send()
        for job in (2, 3, 6, 7):
            done(job)

    for d in range(1, nr):
        piece_copy(d).wait_send()


def body(nr, nc, sigma_anc, owner, structure, factor, diag_inv):
    rows = sigma_anc.shape[1]
    width = factor.shape[2]
    strip = width // nr
    full = factor[0]
    cut = full.reshape(nc, rows, width)
    padded = -(-rows // 16) * 16
    if padded != rows:
        extra = (0, 0), (0, padded - rows), (0, 0)
        sigma_anc, cut = jnp.pad(sigma_anc, extra), jnp.pad(cut, extra)
    vmem = pl.BlockSpec(memory_space=pltpu.VMEM)
    smem = pl.BlockSpec(memory_space=pltpu.SMEM)
    dma = pltpu.SemaphoreType.DMA
    outgoing = pl.pallas_call(
        gather_kernel,
        out_shape=jax.ShapeDtypeStruct((nc, nr * padded, width), jnp.bfloat16),
        in_specs=[smem, smem, vmem],
        out_specs=vmem,
        compiler_params=pltpu.CompilerParams(vmem_limit_bytes=32 * 1024 * 1024),
    )(owner, structure.T, sigma_anc)
    results = (
        jax.ShapeDtypeStruct((nc, padded, width), jnp.bfloat16),
        jax.ShapeDtypeStruct((strip, width), jnp.float32),
    )
    line = nc == 8 and padded == rows and width % (16 * CHUNKS) == 0
    ending = [
        pltpu.VMEM((width, width), jnp.float32),
        pltpu.VMEM((nr - 1, strip, width), jnp.bfloat16),
        pltpu.VMEM((nr - 1, strip, width), jnp.bfloat16),
    ]
    if line:
        run = functools.partial(line_kernel, nr, nc)
        scratch = [
            pltpu.VMEM((nc, width, width), jnp.bfloat16),
            pltpu.VMEM((2, nr * rows, width), jnp.bfloat16),
            pltpu.VMEM((10, nr * rows, width), jnp.bfloat16),
            pltpu.VMEM((nr - 1, 10, rows, width), jnp.bfloat16),
            pltpu.VMEM((10, rows, width), jnp.bfloat16),
            *ending,
            dma((nc, CHUNKS)), dma((nc, CHUNKS)), dma((nc, CHUNKS)), dma((2,)), dma((2,)),
            dma((nr - 1, 10)), dma((nr - 1, 10)), dma((10,)), dma((nc,)), dma((nr - 1,)), dma((nr - 1,)),
        ]
    else:
        run = functools.partial(direct_kernel, nr, nc)
        scratch = [
            pltpu.VMEM((nc, nr * padded, width), jnp.bfloat16),
            pltpu.VMEM((nc, nr * padded, width), jnp.bfloat16),
            pltpu.VMEM((nr - 1, nc, padded, width), jnp.bfloat16),
            *ending,
            dma((nc,)), dma((nc,)), dma((nr - 1, nc)), dma((nr - 1, nc)), dma((nr - 1,)), dma((nr - 1,)),
        ]
    off, diag = pl.pallas_call(
        run,
        out_shape=results,
        in_specs=[vmem, vmem, vmem, vmem],
        out_specs=(vmem, vmem),
        scratch_shapes=scratch,
        compiler_params=pltpu.CompilerParams(
            collective_id=1 if line else 0, has_side_effects=True, vmem_limit_bytes=60 * 1024 * 1024
        ),
    )(outgoing, full, cut, diag_inv[0].T)
    return off[:, :rows].reshape(1, width, width), diag.T[None]


def solution(mesh):
    return jax.shard_map(
        functools.partial(body, mesh.shape["row"], mesh.shape["col"]),
        mesh=mesh,
        in_specs=(P(None, "col", "row"), P(), P(), P("col", "row", None), P("col", None, "row")),
        out_specs=(P("col", "row", None), P("col", None, "row")),
        check_vma=False,
    )
```

```python
import functools

import jax
import jax.numpy as jnp
from jax import lax
from jax.experimental import pallas as pl
from jax.experimental.pallas import tpu as pltpu
from jax.sharding import PartitionSpec as P

MESH = pl.DeviceIdType.MESH


def gather_kernel(owner_ref, struct_ref, sig_ref, out_ref):
    r = lax.axis_index("row")
    rows = sig_ref.shape[1]
    width = out_ref.shape[2]
    groups = sig_ref.shape[2] // width

    @pl.loop(0, struct_ref.shape[1])
    def _(k):
        column = owner_ref[struct_ref[r, k]] - r * groups
        lanes = pl.ds(pl.multiple_of(column * width, 128), width)
        for a in range(struct_ref.shape[0]):
            out_ref[k, a * rows : (a + 1) * rows, :] = sig_ref[struct_ref[a, k], :, lanes]


def direct_kernel(
    nr, nc, outgoing, full_ref, fac_ref, diag_ref, off_ref, out_ref,
    recv, terms, rs_recv, total, pieces, p_recv,
    a_send, a_recv, b_send, b_recv, d_send, d_recv,
):
    r = lax.axis_index("row")
    c = lax.axis_index("col")
    rows = fac_ref.shape[1]
    width = full_ref.shape[1]
    strip = width // nr

    def flipped(s):
        result = 0
        bit = 1
        while bit < nc:
            mine = (c // bit) % 2
            other = (s // bit) % 2
            result = result + bit * (mine + other - 2 * mine * other)
            bit *= 2
        return result

    barrier = pltpu.get_barrier_semaphore()
    for d in range(1, nc):
        pl.semaphore_signal(barrier, inc=1, device_id=(r, lax.rem(c + d, nc)), device_id_type=MESH)
    for d in range(1, nr):
        pl.semaphore_signal(barrier, inc=1, device_id=(lax.rem(r + d, nr), c), device_id_type=MESH)

    def sigma_copy(s):
        k = flipped(s)
        return pltpu.make_async_remote_copy(
            src_ref=outgoing.at[k], dst_ref=recv.at[c], send_sem=a_send.at[k], recv_sem=a_recv.at[c],
            device_id=(r, k), device_id_type=MESH,
        )

    def sigma_wait(k):
        pltpu.make_async_remote_copy(
            src_ref=outgoing.at[k], dst_ref=recv.at[k], send_sem=a_send.at[k], recv_sem=a_recv.at[k],
            device_id=(r, k), device_id_type=MESH,
        ).wait_recv()

    def term_copy(i, d):
        to = lax.rem(r + d, nr)
        return pltpu.make_async_remote_copy(
            src_ref=terms.at[i, pl.ds(to * rows, rows)], dst_ref=rs_recv.at[d - 1, i],
            send_sem=b_send.at[d - 1, i], recv_sem=b_recv.at[d - 1, i],
            device_id=(to, c), device_id_type=MESH,
        )

    def piece_copy(d):
        to = lax.rem(r + d, nr)
        return pltpu.make_async_remote_copy(
            src_ref=pieces.at[d - 1], dst_ref=p_recv.at[d - 1],
            send_sem=d_send.at[d - 1], recv_sem=d_recv.at[d - 1],
            device_id=(to, c), device_id_type=MESH,
        )

    pl.semaphore_wait(barrier, nc - 1 + nr - 1)

    @pl.loop(0, nc - 1)
    def _(t):
        sigma_copy(nc - 1 - t).start()

    total[...] = jnp.zeros_like(total)

    def finish(s):
        i = flipped(s)
        for d in range(1, nr):
            term_copy(i, d).wait_recv()
        acc = terms[i, pl.ds(r * rows, rows)].astype(jnp.float32)
        for d in range(1, nr):
            acc = acc + rs_recv[d - 1, i].astype(jnp.float32)
        block = (-acc).astype(jnp.bfloat16)
        off_ref[i] = block
        total[...] += lax.dot_general(
            block, fac_ref[i], (((0,), (0,)), ((), ())), preferred_element_type=jnp.float32
        )

    @pl.loop(0, nc)
    def _(s):
        i = flipped(s)

        @pl.when(s > 0)
        def _():
            sigma_wait(i)

        def multiply(block):
            product = jnp.dot(block, full_ref[...], preferred_element_type=jnp.float32)
            terms[i] = product.astype(jnp.bfloat16)

        @pl.when(s == 0)
        def _():
            multiply(outgoing[c])

        @pl.when(s > 0)
        def _():
            multiply(recv[i])

        for d in range(1, nr):
            term_copy(i, d).start()

        @pl.when(s > 0)
        def _():
            finish(s - 1)

    finish(nc - 1)
    for d in range(1, nr):
        to = lax.rem(r + d, nr)
        pieces[d - 1] = total[pl.ds(pl.multiple_of(to * strip, 8), strip), :].astype(jnp.bfloat16)
        piece_copy(d).start()
    acc = total[pl.ds(pl.multiple_of(r * strip, 8), strip), :]
    for d in range(1, nr):
        piece_copy(d).wait_recv()
        acc = acc + p_recv[d - 1].astype(jnp.float32)
    out_ref[...] = diag_ref[...] - acc

    @pl.loop(1, nc)
    def _(s):
        sigma_copy(s).wait_send()

    @pl.loop(0, nc)
    def _(i):
        for d in range(1, nr):
            term_copy(i, d).wait_send()

    for d in range(1, nr):
        piece_copy(d).wait_send()


CHUNKS = 4


def line_kernel(
    nr, nc, outgoing, full_ref, diag_ref, off_ref, out_ref,
    panels, diag_here, sent_rows, terms, rs_recv, stage, total, pieces, p_recv,
    z_send, s_send, g_recv, a_send, a_recv, b_send, b_recv, o_send, o_recv, d_send, d_recv, load,
):
    r = lax.axis_index("row")
    c = lax.axis_index("col")
    rows = outgoing.shape[1] // nr
    width = full_ref.shape[1]
    strip = width // nr
    depth = width // CHUNKS
    z, q = c // 2, c % 2
    half = z // 2
    mid, end = 2 * (1 + half), 6 * half
    mid_far, end_far = 2 * (2 - half), 6 * (1 - half)
    here = 2 * z
    sibling = here + 1 - q
    is_end = 1 - (z + 1) // 2 % 2

    load_panel = pltpu.make_async_copy(full_ref, panels.at[c], load.at[0])
    load_panel.start()
    load_diag = pltpu.make_async_copy(diag_ref, diag_here, load.at[1])
    load_diag.start()

    barrier = pltpu.get_barrier_semaphore()
    for d in range(1, nc):
        pl.semaphore_signal(barrier, inc=1, device_id=(r, lax.rem(c + d, nc)), device_id_type=MESH)
    for d in range(1, nr):
        pl.semaphore_signal(barrier, inc=1, device_id=(lax.rem(r + d, nr), c), device_id_type=MESH)

    def panel_copy(k, ch, to, sem):
        part = panels.at[k, pl.ds(ch * depth, depth)]
        return pltpu.make_async_remote_copy(
            src_ref=part, dst_ref=part, send_sem=sem.at[k, ch], recv_sem=g_recv.at[k, ch],
            device_id=(r, to), device_id_type=MESH,
        )

    def to_sibling(k, ch):
        return panel_copy(k, ch, sibling, s_send)

    def take(k, ch, onward=None):
        panel_copy(k, ch, sibling, s_send).wait_recv()
        if onward is not None:
            panel_copy(k, ch, onward, z_send).start()
        to_sibling(k, ch).start()

    def from_sibling(k):
        @pl.loop(0, CHUNKS)
        def _(ch):
            to_sibling(k, ch).wait_recv()

    def rows_copy(t):
        return pltpu.make_async_remote_copy(
            src_ref=outgoing.at[mid + t], dst_ref=sent_rows.at[q], send_sem=a_send.at[t], recv_sem=a_recv.at[q],
            device_id=(r, mid + t), device_id_type=MESH,
        )

    def rows_wait(t):
        pltpu.make_async_remote_copy(
            src_ref=outgoing.at[mid + t], dst_ref=sent_rows.at[t], send_sem=a_send.at[t], recv_sem=a_recv.at[t],
            device_id=(r, end + t), device_id_type=MESH,
        ).wait_recv()

    def term_copy(job, d):
        to = lax.rem(r + d, nr)
        return pltpu.make_async_remote_copy(
            src_ref=terms.at[job, pl.ds(to * rows, rows)], dst_ref=rs_recv.at[d - 1, job],
            send_sem=b_send.at[d - 1, job], recv_sem=b_recv.at[d - 1, job],
            device_id=(to, c), device_id_type=MESH,
        )

    def tile_copy(job, k):
        return pltpu.make_async_remote_copy(
            src_ref=stage.at[job], dst_ref=off_ref.at[c], send_sem=o_send.at[job], recv_sem=o_recv.at[c],
            device_id=(r, k), device_id_type=MESH,
        )

    def tile_wait(i):
        pltpu.make_async_remote_copy(
            src_ref=stage.at[0], dst_ref=off_ref.at[i], send_sem=o_send.at[0], recv_sem=o_recv.at[i],
            device_id=(r, i), device_id_type=MESH,
        ).wait_recv()

    def piece_copy(d):
        to = lax.rem(r + d, nr)
        return pltpu.make_async_remote_copy(
            src_ref=pieces.at[d - 1], dst_ref=p_recv.at[d - 1],
            send_sem=d_send.at[d - 1], recv_sem=d_recv.at[d - 1],
            device_id=(to, c), device_id_type=MESH,
        )

    def multiply(job, left, right):
        product = jnp.dot(left[...], right[...], preferred_element_type=jnp.float32)
        terms[job] = product.astype(jnp.bfloat16)
        for d in range(1, nr):
            term_copy(job, d).start()

    def issue(group, base):
        @pl.loop(0, 2)
        def _(t):
            k = base + (q + t) % 2

            @pl.when(t == 1)
            def _():
                from_sibling(k)

            multiply(2 * group + t, outgoing.at[k], panels.at[k])

    def summed(job):
        for d in range(1, nr):
            term_copy(job, d).wait_recv()
        acc = terms[job, pl.ds(pl.multiple_of(r * rows, 16), rows)].astype(jnp.float32)
        for d in range(1, nr):
            acc = acc + rs_recv[d - 1, job].astype(jnp.float32)
        return (-acc).astype(jnp.bfloat16)

    def deliver(group, base):
        @pl.loop(0, 2)
        def _(t):
            job = 2 * group + t
            stage[job] = summed(job)
            tile_copy(job, base + (q + t) % 2).start()

    def deliver_own():
        off_ref[c] = summed(0)
        stage[1] = summed(1)
        tile_copy(1, sibling).start()

    pl.semaphore_wait(barrier, nc - 1 + nr - 1)

    @pl.when(is_end == 1)
    def _():
        rows_copy(q).start()

    load_panel.wait()

    @pl.loop(0, CHUNKS)
    def _(ch):
        panel_copy(c, ch, (1 - is_end) * mid_far + is_end * mid + q, z_send).start()
        to_sibling(c, ch).start()

    issue(0, here)

    @pl.when(is_end == 1)
    def _():
        @pl.loop(0, CHUNKS)
        def _(ch):
            panel_copy(c, ch, mid + q, z_send).wait_send()

        rows_copy(1 - q).start()

        @pl.loop(0, CHUNKS)
        def _(ch):
            take(mid_far + q, ch)

        deliver_own()

    @pl.when(is_end == 0)
    def _():
        take(mid_far + q, 0, end + q)
        rows_wait(q)
        multiply(6, sent_rows.at[q], panels.at[c])
        take(mid_far + q, 1, end + q)
        take(end + q, 0, mid_far + q)
        take(mid_far + q, 2, end + q)
        deliver_own()
        take(end + q, 1, mid_far + q)
        take(mid_far + q, 3, end + q)

    issue(2, mid_far)

    @pl.when(is_end == 1)
    def _():
        deliver(2, mid_far)

        @pl.loop(0, CHUNKS)
        def _(ch):
            take(end_far + q, ch)

    @pl.when(is_end == 0)
    def _():
        take(end + q, 2, mid_far + q)
        take(end + q, 3, mid_far + q)
        issue(1, end)
        take(end_far + q, 0, end + q)
        deliver(2, mid_far)
        take(end_far + q, 1, end + q)
        take(end_far + q, 2, end + q)
        deliver(1, end)
        take(end_far + q, 3, end + q)

    issue(4, end_far)

    @pl.when(is_end == 0)
    def _():
        rows_wait(1 - q)
        multiply(7, sent_rows.at[1 - q], panels.at[c])

    deliver(4, end_far)

    @pl.when(is_end == 0)
    def _():
        @pl.loop(0, 2)
        def _(t):
            off_ref[end + (q + t) % 2] = summed(6 + t)

    def partial(start):
        part = pl.ds(start, nc // 2)
        return lax.dot_general(
            off_ref[part].reshape(width // 2, width),
            panels[c, pl.ds(pl.multiple_of(start * rows, 16), width // 2)],
            (((0,), (0,)), ((), ())), preferred_element_type=jnp.float32,
        )

    tile_wait(sibling)

    @pl.when(is_end == 1)
    def _():
        tile_wait(mid)
        tile_wait(mid + 1)

    total[...] = partial(half * (nc // 2))
    for i in (mid_far, mid_far + 1, end_far, end_far + 1):
        tile_wait(i)
    total[...] += partial((1 - half) * (nc // 2))

    for d in range(1, nr):
        to = lax.rem(r + d, nr)
        pieces[d - 1] = total[pl.ds(pl.multiple_of(to * strip, 8), strip), :].astype(jnp.bfloat16)
        piece_copy(d).start()
    acc = total[pl.ds(pl.multiple_of(r * strip, 8), strip), :]
    for d in range(1, nr):
        piece_copy(d).wait_recv()
        acc = acc + p_recv[d - 1].astype(jnp.float32)
    load_diag.wait()
    out_ref[...] = diag_here[...] - acc

    def sent(base):
        @pl.loop(0, CHUNKS)
        def _(ch):
            panel_copy(base, ch, sibling, z_send).wait_send()

    def shared(base):
        @pl.loop(0, CHUNKS)
        def _(ch):
            to_sibling(base, ch).wait_send()

    def done(job):
        for d in range(1, nr):
            term_copy(job, d).wait_send()

    for k in (c, mid_far + q, end_far + q):
        shared(k)
    tile_copy(1, sibling).wait_send()
    for group in (2, 4):
        for t in range(2):
            tile_copy(2 * group + t, sibling).wait_send()
    for job in (0, 1, 4, 5, 8, 9):
        done(job)

    @pl.when(is_end == 1)
    def _():
        for t in range(2):
            rows_copy(t).wait_send()

    @pl.when(is_end == 0)
    def _():
        for k in (c, end + q, mid_far + q, end_far + q):
            sent(k)
        shared(end + q)
        for t in range(2):
            tile_copy(2 + t, sibling).wait_send()
        for job in (2, 3, 6, 7):
            done(job)

    for d in range(1, nr):
        piece_copy(d).wait_send()


def body(nr, nc, sigma_anc, owner, structure, factor, diag_inv):
    rows = sigma_anc.shape[1]
    width = factor.shape[2]
    strip = width // nr
    full = factor[0]
    cut = full.reshape(nc, rows, width)
    padded = -(-rows // 16) * 16
    if padded != rows:
        extra = (0, 0), (0, padded - rows), (0, 0)
        sigma_anc, cut = jnp.pad(sigma_anc, extra), jnp.pad(cut, extra)
    vmem = pl.BlockSpec(memory_space=pltpu.VMEM)
    smem = pl.BlockSpec(memory_space=pltpu.SMEM)
    dma = pltpu.SemaphoreType.DMA
    outgoing = pl.pallas_call(
        gather_kernel,
        out_shape=jax.ShapeDtypeStruct((nc, nr * padded, width), jnp.bfloat16),
        in_specs=[smem, smem, vmem],
        out_specs=vmem,
        compiler_params=pltpu.CompilerParams(vmem_limit_bytes=24 * 1024 * 1024),
    )(owner, structure.T, sigma_anc)
    results = (
        jax.ShapeDtypeStruct((nc, padded, width), jnp.bfloat16),
        jax.ShapeDtypeStruct((strip, width), jnp.float32),
    )
    line = nc == 8 and padded == rows and width % (16 * CHUNKS) == 0
    ending = [
        pltpu.VMEM((width, width), jnp.float32),
        pltpu.VMEM((nr - 1, strip, width), jnp.bfloat16),
        pltpu.VMEM((nr - 1, strip, width), jnp.bfloat16),
    ]
    anywhere = pl.BlockSpec(memory_space=pl.ANY)
    if line:
        operands, places = (outgoing, full, diag_inv[0].T), [vmem, anywhere, anywhere]
        run = functools.partial(line_kernel, nr, nc)
        scratch = [
            pltpu.VMEM((nc, width, width), jnp.bfloat16),
            pltpu.VMEM((strip, width), jnp.float32),
            pltpu.VMEM((2, nr * rows, width), jnp.bfloat16),
            pltpu.VMEM((10, nr * rows, width), jnp.bfloat16),
            pltpu.VMEM((nr - 1, 10, rows, width), jnp.bfloat16),
            pltpu.VMEM((10, rows, width), jnp.bfloat16),
            *ending,
            dma((nc, CHUNKS)), dma((nc, CHUNKS)), dma((nc, CHUNKS)), dma((2,)), dma((2,)),
            dma((nr - 1, 10)), dma((nr - 1, 10)), dma((10,)), dma((nc,)), dma((nr - 1,)), dma((nr - 1,)), dma((2,)),
        ]
    else:
        operands, places = (outgoing, full, cut, diag_inv[0].T), [vmem] * 4
        run = functools.partial(direct_kernel, nr, nc)
        scratch = [
            pltpu.VMEM((nc, nr * padded, width), jnp.bfloat16),
            pltpu.VMEM((nc, nr * padded, width), jnp.bfloat16),
            pltpu.VMEM((nr - 1, nc, padded, width), jnp.bfloat16),
            *ending,
            dma((nc,)), dma((nc,)), dma((nr - 1, nc)), dma((nr - 1, nc)), dma((nr - 1,)), dma((nr - 1,)),
        ]
    off, diag = pl.pallas_call(
        run,
        out_shape=results,
        in_specs=places,
        out_specs=(vmem, vmem),
        scratch_shapes=scratch,
        compiler_params=pltpu.CompilerParams(
            collective_id=1 if line else 0, has_side_effects=True, vmem_limit_bytes=(32 if line else 60) * 1024 * 1024
        ),
    )(*operands)
    return off[:, :rows].reshape(1, width, width), diag.T[None]


def solution(mesh):
    return jax.shard_map(
        functools.partial(body, mesh.shape["row"], mesh.shape["col"]),
        mesh=mesh,
        in_specs=(P(None, "col", "row"), P(), P(), P("col", "row", None), P("col", None, "row")),
        out_specs=(P("col", "row", None), P("col", None, "row")),
        check_vma=False,
    )
```

```python
import functools

import jax
import jax.numpy as jnp
from jax import lax
from jax.experimental import pallas as pl
from jax.experimental.pallas import tpu as pltpu
from jax.sharding import PartitionSpec as P

MESH = pl.DeviceIdType.MESH


def gather_kernel(owner_ref, struct_ref, sig_ref, out_ref):
    r = lax.axis_index("row")
    rows = sig_ref.shape[1]
    width = out_ref.shape[2]
    groups = sig_ref.shape[2] // width

    @pl.loop(0, struct_ref.shape[1])
    def _(k):
        column = owner_ref[struct_ref[r, k]] - r * groups
        lanes = pl.ds(pl.multiple_of(column * width, 128), width)
        for a in range(struct_ref.shape[0]):
            out_ref[k, a * rows : (a + 1) * rows, :] = sig_ref[struct_ref[a, k], :, lanes]


def direct_kernel(
    nr, nc, outgoing, full_ref, fac_ref, diag_ref, off_ref, out_ref,
    recv, terms, rs_recv, total, pieces, p_recv,
    a_send, a_recv, b_send, b_recv, d_send, d_recv,
):
    r = lax.axis_index("row")
    c = lax.axis_index("col")
    rows = fac_ref.shape[1]
    width = full_ref.shape[1]
    strip = width // nr

    def flipped(s):
        result = 0
        bit = 1
        while bit < nc:
            mine = (c // bit) % 2
            other = (s // bit) % 2
            result = result + bit * (mine + other - 2 * mine * other)
            bit *= 2
        return result

    barrier = pltpu.get_barrier_semaphore()
    for d in range(1, nc):
        pl.semaphore_signal(barrier, inc=1, device_id=(r, lax.rem(c + d, nc)), device_id_type=MESH)
    for d in range(1, nr):
        pl.semaphore_signal(barrier, inc=1, device_id=(lax.rem(r + d, nr), c), device_id_type=MESH)

    def sigma_copy(s):
        k = flipped(s)
        return pltpu.make_async_remote_copy(
            src_ref=outgoing.at[k], dst_ref=recv.at[c], send_sem=a_send.at[k], recv_sem=a_recv.at[c],
            device_id=(r, k), device_id_type=MESH,
        )

    def sigma_wait(k):
        pltpu.make_async_remote_copy(
            src_ref=outgoing.at[k], dst_ref=recv.at[k], send_sem=a_send.at[k], recv_sem=a_recv.at[k],
            device_id=(r, k), device_id_type=MESH,
        ).wait_recv()

    def term_copy(i, d):
        to = lax.rem(r + d, nr)
        return pltpu.make_async_remote_copy(
            src_ref=terms.at[i, pl.ds(to * rows, rows)], dst_ref=rs_recv.at[d - 1, i],
            send_sem=b_send.at[d - 1, i], recv_sem=b_recv.at[d - 1, i],
            device_id=(to, c), device_id_type=MESH,
        )

    def piece_copy(d):
        to = lax.rem(r + d, nr)
        return pltpu.make_async_remote_copy(
            src_ref=pieces.at[d - 1], dst_ref=p_recv.at[d - 1],
            send_sem=d_send.at[d - 1], recv_sem=d_recv.at[d - 1],
            device_id=(to, c), device_id_type=MESH,
        )

    pl.semaphore_wait(barrier, nc - 1 + nr - 1)

    @pl.loop(0, nc - 1)
    def _(t):
        sigma_copy(nc - 1 - t).start()

    total[...] = jnp.zeros_like(total)

    def finish(s):
        i = flipped(s)
        for d in range(1, nr):
            term_copy(i, d).wait_recv()
        acc = terms[i, pl.ds(r * rows, rows)].astype(jnp.float32)
        for d in range(1, nr):
            acc = acc + rs_recv[d - 1, i].astype(jnp.float32)
        block = (-acc).astype(jnp.bfloat16)
        off_ref[i] = block
        total[...] += lax.dot_general(
            block, fac_ref[i], (((0,), (0,)), ((), ())), preferred_element_type=jnp.float32
        )

    @pl.loop(0, nc)
    def _(s):
        i = flipped(s)

        @pl.when(s > 0)
        def _():
            sigma_wait(i)

        def multiply(block):
            product = jnp.dot(block, full_ref[...], preferred_element_type=jnp.float32)
            terms[i] = product.astype(jnp.bfloat16)

        @pl.when(s == 0)
        def _():
            multiply(outgoing[c])

        @pl.when(s > 0)
        def _():
            multiply(recv[i])

        for d in range(1, nr):
            term_copy(i, d).start()

        @pl.when(s > 0)
        def _():
            finish(s - 1)

    finish(nc - 1)
    for d in range(1, nr):
        to = lax.rem(r + d, nr)
        pieces[d - 1] = total[pl.ds(pl.multiple_of(to * strip, 8), strip), :].astype(jnp.bfloat16)
        piece_copy(d).start()
    acc = total[pl.ds(pl.multiple_of(r * strip, 8), strip), :]
    for d in range(1, nr):
        piece_copy(d).wait_recv()
        acc = acc + p_recv[d - 1].astype(jnp.float32)
    out_ref[...] = diag_ref[...] - acc

    @pl.loop(1, nc)
    def _(s):
        sigma_copy(s).wait_send()

    @pl.loop(0, nc)
    def _(i):
        for d in range(1, nr):
            term_copy(i, d).wait_send()

    for d in range(1, nr):
        piece_copy(d).wait_send()


CHUNKS = 4


def line_kernel(
    nr, nc, outgoing, full_ref, diag_ref, off_ref, out_ref,
    panels, diag_here, sent_rows, terms, rs_recv, stage, total, pieces, p_recv,
    z_send, s_send, g_recv, a_send, a_recv, b_send, b_recv, o_send, o_recv, d_send, d_recv, load,
):
    r = lax.axis_index("row")
    c = lax.axis_index("col")
    rows = outgoing.shape[1] // nr
    width = full_ref.shape[1]
    strip = width // nr
    depth = width // CHUNKS
    z, q = c // 2, c % 2
    half = z // 2
    mid, end = 2 * (1 + half), 6 * half
    mid_far, end_far = 2 * (2 - half), 6 * (1 - half)
    here = 2 * z
    sibling = here + 1 - q
    is_end = 1 - (z + 1) // 2 % 2

    load_panel = pltpu.make_async_copy(full_ref, panels.at[c], load.at[0])
    load_panel.start()
    load_diag = pltpu.make_async_copy(diag_ref, diag_here, load.at[1])
    load_diag.start()

    barrier = pltpu.get_barrier_semaphore()
    for d in range(1, nc):
        pl.semaphore_signal(barrier, inc=1, device_id=(r, lax.rem(c + d, nc)), device_id_type=MESH)
    for d in range(1, nr):
        pl.semaphore_signal(barrier, inc=1, device_id=(lax.rem(r + d, nr), c), device_id_type=MESH)

    def panel_copy(k, ch, to, sem):
        part = panels.at[k, pl.ds(ch * depth, depth)]
        return pltpu.make_async_remote_copy(
            src_ref=part, dst_ref=part, send_sem=sem.at[k, ch], recv_sem=g_recv.at[k, ch],
            device_id=(r, to), device_id_type=MESH,
        )

    def to_sibling(k, ch):
        return panel_copy(k, ch, sibling, s_send)

    def take(k, ch, onward=None):
        panel_copy(k, ch, sibling, s_send).wait_recv()
        if onward is not None:
            panel_copy(k, ch, onward, z_send).start()
        to_sibling(k, ch).start()

    def from_sibling(k):
        @pl.loop(0, CHUNKS)
        def _(ch):
            to_sibling(k, ch).wait_recv()

    def rows_copy(t):
        return pltpu.make_async_remote_copy(
            src_ref=outgoing.at[mid + t], dst_ref=sent_rows.at[q], send_sem=a_send.at[t], recv_sem=a_recv.at[q],
            device_id=(r, mid + t), device_id_type=MESH,
        )

    def rows_wait(t):
        pltpu.make_async_remote_copy(
            src_ref=outgoing.at[mid + t], dst_ref=sent_rows.at[t], send_sem=a_send.at[t], recv_sem=a_recv.at[t],
            device_id=(r, end + t), device_id_type=MESH,
        ).wait_recv()

    def term_copy(job, d):
        to = lax.rem(r + d, nr)
        return pltpu.make_async_remote_copy(
            src_ref=terms.at[job, pl.ds(to * rows, rows)], dst_ref=rs_recv.at[d - 1, job],
            send_sem=b_send.at[d - 1, job], recv_sem=b_recv.at[d - 1, job],
            device_id=(to, c), device_id_type=MESH,
        )

    def tile_copy(job, k):
        return pltpu.make_async_remote_copy(
            src_ref=stage.at[job], dst_ref=off_ref.at[c], send_sem=o_send.at[job], recv_sem=o_recv.at[c],
            device_id=(r, k), device_id_type=MESH,
        )

    def tile_wait(i):
        pltpu.make_async_remote_copy(
            src_ref=stage.at[0], dst_ref=off_ref.at[i], send_sem=o_send.at[0], recv_sem=o_recv.at[i],
            device_id=(r, i), device_id_type=MESH,
        ).wait_recv()

    def piece_copy(d):
        to = lax.rem(r + d, nr)
        return pltpu.make_async_remote_copy(
            src_ref=pieces.at[d - 1], dst_ref=p_recv.at[d - 1],
            send_sem=d_send.at[d - 1], recv_sem=d_recv.at[d - 1],
            device_id=(to, c), device_id_type=MESH,
        )

    def multiply(job, left, right):
        product = jnp.dot(left[...], right[...], preferred_element_type=jnp.float32)
        terms[job] = product.astype(jnp.bfloat16)
        for d in range(1, nr):
            term_copy(job, d).start()

    def issue(group, base):
        @pl.loop(0, 2)
        def _(t):
            k = base + (q + t) % 2

            @pl.when(t == 1)
            def _():
                from_sibling(k)

            multiply(2 * group + t, outgoing.at[k], panels.at[k])

    def summed(job):
        for d in range(1, nr):
            term_copy(job, d).wait_recv()
        acc = terms[job, pl.ds(pl.multiple_of(r * rows, 16), rows)].astype(jnp.float32)
        for d in range(1, nr):
            acc = acc + rs_recv[d - 1, job].astype(jnp.float32)
        return (-acc).astype(jnp.bfloat16)

    def deliver(group, base):
        @pl.loop(0, 2)
        def _(t):
            job = 2 * group + t
            stage[job] = summed(job)
            tile_copy(job, base + (q + t) % 2).start()

    def deliver_own():
        off_ref[c] = summed(0)
        stage[1] = summed(1)
        tile_copy(1, sibling).start()

    pl.semaphore_wait(barrier, nc - 1 + nr - 1)

    load_panel.wait()

    @pl.loop(0, CHUNKS)
    def _(ch):
        panel_copy(c, ch, (1 - is_end) * mid_far + is_end * mid + q, z_send).start()
        to_sibling(c, ch).start()

    issue(0, here)

    @pl.when(is_end == 1)
    def _():
        @pl.loop(0, CHUNKS)
        def _(ch):
            panel_copy(c, ch, mid + q, z_send).wait_send()

        @pl.loop(0, 2)
        def _(t):
            rows_copy(t).start()

        @pl.loop(0, CHUNKS)
        def _(ch):
            take(mid_far + q, ch)

    @pl.when(is_end == 0)
    def _():
        @pl.loop(0, CHUNKS)
        def _(ch):
            take(end + q, ch, mid_far + q)
            take(mid_far + q, ch, end + q)

        issue(1, end)

    issue(2, mid_far)
    deliver_own()

    @pl.when(is_end == 1)
    def _():
        deliver(2, mid_far)

        @pl.loop(0, CHUNKS)
        def _(ch):
            take(end_far + q, ch)

    @pl.when(is_end == 0)
    def _():
        take(end_far + q, 0, end + q)
        take(end_far + q, 1, end + q)
        deliver(1, end)
        take(end_far + q, 2, end + q)
        deliver(2, mid_far)
        take(end_far + q, 3, end + q)

    issue(4, end_far)

    @pl.when(is_end == 0)
    def _():
        @pl.loop(0, 2)
        def _(t):
            rows_wait(t)
            multiply(6 + t, sent_rows.at[t], panels.at[c])

    deliver(4, end_far)

    @pl.when(is_end == 0)
    def _():
        @pl.loop(0, 2)
        def _(t):
            off_ref[end + t] = summed(6 + t)

    def partial(start):
        part = pl.ds(start, nc // 2)
        return lax.dot_general(
            off_ref[part].reshape(width // 2, width),
            panels[c, pl.ds(pl.multiple_of(start * rows, 16), width // 2)],
            (((0,), (0,)), ((), ())), preferred_element_type=jnp.float32,
        )

    tile_wait(sibling)

    @pl.when(is_end == 1)
    def _():
        tile_wait(mid)
        tile_wait(mid + 1)

    total[...] = partial(half * (nc // 2))
    for i in (mid_far, mid_far + 1, end_far, end_far + 1):
        tile_wait(i)
    total[...] += partial((1 - half) * (nc // 2))

    for d in range(1, nr):
        to = lax.rem(r + d, nr)
        pieces[d - 1] = total[pl.ds(pl.multiple_of(to * strip, 8), strip), :].astype(jnp.bfloat16)
        piece_copy(d).start()
    acc = total[pl.ds(pl.multiple_of(r * strip, 8), strip), :]
    for d in range(1, nr):
        piece_copy(d).wait_recv()
        acc = acc + p_recv[d - 1].astype(jnp.float32)
    load_diag.wait()
    out_ref[...] = diag_here[...] - acc

    def sent(base):
        @pl.loop(0, CHUNKS)
        def _(ch):
            panel_copy(base, ch, sibling, z_send).wait_send()

    def shared(base):
        @pl.loop(0, CHUNKS)
        def _(ch):
            to_sibling(base, ch).wait_send()

    def done(job):
        for d in range(1, nr):
            term_copy(job, d).wait_send()

    for k in (c, mid_far + q, end_far + q):
        shared(k)
    tile_copy(1, sibling).wait_send()
    for group in (2, 4):
        for t in range(2):
            tile_copy(2 * group + t, sibling).wait_send()
    for job in (0, 1, 4, 5, 8, 9):
        done(job)

    @pl.when(is_end == 1)
    def _():
        for t in range(2):
            rows_copy(t).wait_send()

    @pl.when(is_end == 0)
    def _():
        for k in (c, end + q, mid_far + q, end_far + q):
            sent(k)
        shared(end + q)
        for t in range(2):
            tile_copy(2 + t, sibling).wait_send()
        for job in (2, 3, 6, 7):
            done(job)

    for d in range(1, nr):
        piece_copy(d).wait_send()


def body(nr, nc, sigma_anc, owner, structure, factor, diag_inv):
    rows = sigma_anc.shape[1]
    width = factor.shape[2]
    strip = width // nr
    full = factor[0]
    cut = full.reshape(nc, rows, width)
    padded = -(-rows // 16) * 16
    if padded != rows:
        extra = (0, 0), (0, padded - rows), (0, 0)
        sigma_anc, cut = jnp.pad(sigma_anc, extra), jnp.pad(cut, extra)
    vmem = pl.BlockSpec(memory_space=pltpu.VMEM)
    smem = pl.BlockSpec(memory_space=pltpu.SMEM)
    dma = pltpu.SemaphoreType.DMA
    outgoing = pl.pallas_call(
        gather_kernel,
        out_shape=jax.ShapeDtypeStruct((nc, nr * padded, width), jnp.bfloat16),
        in_specs=[smem, smem, vmem],
        out_specs=vmem,
        compiler_params=pltpu.CompilerParams(vmem_limit_bytes=24 * 1024 * 1024),
    )(owner, structure.T, sigma_anc)
    results = (
        jax.ShapeDtypeStruct((nc, padded, width), jnp.bfloat16),
        jax.ShapeDtypeStruct((strip, width), jnp.float32),
    )
    line = nc == 8 and padded == rows and width % (16 * CHUNKS) == 0
    ending = [
        pltpu.VMEM((width, width), jnp.float32),
        pltpu.VMEM((nr - 1, strip, width), jnp.bfloat16),
        pltpu.VMEM((nr - 1, strip, width), jnp.bfloat16),
    ]
    anywhere = pl.BlockSpec(memory_space=pl.ANY)
    if line:
        operands, places = (outgoing, full, diag_inv[0].T), [vmem, anywhere, anywhere]
        run = functools.partial(line_kernel, nr, nc)
        scratch = [
            pltpu.VMEM((nc, width, width), jnp.bfloat16),
            pltpu.VMEM((strip, width), jnp.float32),
            pltpu.VMEM((2, nr * rows, width), jnp.bfloat16),
            pltpu.VMEM((10, nr * rows, width), jnp.bfloat16),
            pltpu.VMEM((nr - 1, 10, rows, width), jnp.bfloat16),
            pltpu.VMEM((10, rows, width), jnp.bfloat16),
            *ending,
            dma((nc, CHUNKS)), dma((nc, CHUNKS)), dma((nc, CHUNKS)), dma((2,)), dma((2,)),
            dma((nr - 1, 10)), dma((nr - 1, 10)), dma((10,)), dma((nc,)), dma((nr - 1,)), dma((nr - 1,)), dma((2,)),
        ]
    else:
        operands, places = (outgoing, full, cut, diag_inv[0].T), [vmem] * 4
        run = functools.partial(direct_kernel, nr, nc)
        scratch = [
            pltpu.VMEM((nc, nr * padded, width), jnp.bfloat16),
            pltpu.VMEM((nc, nr * padded, width), jnp.bfloat16),
            pltpu.VMEM((nr - 1, nc, padded, width), jnp.bfloat16),
            *ending,
            dma((nc,)), dma((nc,)), dma((nr - 1, nc)), dma((nr - 1, nc)), dma((nr - 1,)), dma((nr - 1,)),
        ]
    off, diag = pl.pallas_call(
        run,
        out_shape=results,
        in_specs=places,
        out_specs=(vmem, vmem),
        scratch_shapes=scratch,
        compiler_params=pltpu.CompilerParams(
            collective_id=1 if line else 0, has_side_effects=True, vmem_limit_bytes=(32 if line else 60) * 1024 * 1024
        ),
    )(*operands)
    return off[:, :rows].reshape(1, width, width), diag.T[None]


def solution(mesh):
    return jax.shard_map(
        functools.partial(body, mesh.shape["row"], mesh.shape["col"]),
        mesh=mesh,
        in_specs=(P(None, "col", "row"), P(), P(), P("col", "row", None), P("col", None, "row")),
        out_specs=(P("col", "row", None), P("col", None, "row")),
        check_vma=False,
    )
```
